256 devices in a mesh: ctx: 16 (over y_lo, x, core), head: 16 (over y_hi, z).
Axes of the slice: x: 4, y: 4 (y_hi: 2, y_lo: 2; y = y_hi * 2 + y_lo), z: 8, core: 2. Of those that a mesh axis runs over, the one named last changes fastest.
Arguments:
- layer_input: bfloat16 [5120, 5120], P('ctx', 'head'), may hold values from -0.29882812 to 0.29882812
- query_heads: bfloat16 [5120, 4096], P('ctx', 'head'), may hold values from -8 to 8
- key_heads: bfloat16 [5120, 4096], P('ctx', 'head'), may hold values from -8 to 8
- value_heads: bfloat16 [5120, 4096], P('ctx', 'head'), may hold values from -6 to 6
- map_one_out: bfloat16 [5120, 4096], P('ctx', 'head'), may hold values from -3 to 3
- map_two_out: bfloat16 [5120, 4096], P('ctx', 'head'), may hold values from -3 to 3
- grad_out: bfloat16 [5120, 4096], P('ctx', 'head'), may hold values from -6 to 6
- saved_lse: float32 [2, 16, 5120], P(None, 'head', 'ctx'), as said below
- lambdas: float32 [16], P('head'), may hold values from 0.2 to 0.8
- block_order: int32 [16], replicated, may hold values from 0 to 15, as said below
Outputs:
- grad_query: bfloat16 [5120, 4096], P('ctx', 'head')
- grad_key: bfloat16 [5120, 4096], P('ctx', 'head')
- grad_value: bfloat16 [5120, 4096], P('ctx', 'head')
- weight_grad: float32 [3, 5120, 4096], P(None, 'ctx', 'head')
The draws below stay inside these ranges and needn't reach their ends.
Inputs may be any that keep to these rules, and one draw needn't show every extreme that they name: `block_order`: a permutation of 0 to 15. saved_lse[m, h, r] is the natural logarithm of the sum, over the keys visible to token r, of exp of the map m scores of head h, q_m k_m^T / sqrt(128).
All inputs are finite; a program needn't handle non-finite values.
Results may differ from the reference program's by a relative error of at most 0.005.
Values may be sent and summed in bfloat16 or wider, within the bound.
A program may use at most 64 MiB of HBM per device.

```python
import math
import jax
import jax.numpy as jnp
from jax import lax

D = 5120
HALF = 128
TOK_DEV = 320
HEADS = 16
TOKENS = 5120
N_CTX = 16


def order_draw(key):
    return jax.random.permutation(jax.random.fold_in(key, 101), N_CTX).astype(jnp.int32)


def pair_draw(key, scale_low, scale_high):
    outputs = []
    for salt_value in (102, 103):
        sub_key = jax.random.fold_in(key, salt_value)
        key_bell = jax.random.fold_in(sub_key, 0)
        key_scale = jax.random.fold_in(sub_key, 2)
        bell_part = jax.random.normal(key_bell, (TOKENS, HEADS * 2 * HALF), jnp.float32)
        row_scale = jnp.exp(jax.random.uniform(key_scale, (TOKENS, 1), jnp.float32, math.log(scale_low), math.log(scale_high)))
        mixed_draw = bell_part * row_scale
        outputs.append(jnp.clip(mixed_draw, -8.0, 8.0).astype(jnp.bfloat16))
    return (outputs[0], outputs[1])


def draw_query_heads(key, part):
    queries, key_rows = pair_draw(key, 1.0, 1.0)
    return queries


def draw_key_heads(key, part):
    queries, key_rows = pair_draw(key, 1.0, 1.0)
    return key_rows


def draw_block_order(key, part):
    order_out = order_draw(key)
    return order_out


def draw_saved_lse(key, part):
    queries, key_rows = pair_draw(key, 1.0, 1.0)
    order_out = order_draw(key)
    row_index = jnp.arange(TOKENS, dtype=jnp.int32)
    positions = order_out[row_index // TOK_DEV] * TOK_DEV + row_index % TOK_DEV
    visible = positions[None, :] <= positions[:, None]
    query_stack = jnp.transpose(queries.astype(jnp.float32).reshape(TOKENS, HEADS, 2 * HALF), (1, 0, 2))
    key_stack = jnp.transpose(key_rows.astype(jnp.float32).reshape(TOKENS, HEADS, 2 * HALF), (1, 0, 2))

    def per_head(pair_items):
        query_part, key_part = pair_items
        results = []
        for offset in (0, HALF):
            scores = jnp.dot(query_part[:, offset:offset + HALF], key_part[:, offset:offset + HALF].T, precision=lax.Precision.HIGHEST) * 0.08838834764831845
            scores = jnp.where(visible, scores, -1e+30)
            row_max = jnp.max(scores, axis=1)
            results.append(row_max + jnp.log(jnp.sum(jnp.exp(scores - row_max[:, None]), axis=1)))
        return jnp.stack(results)
    stacked = lax.map(per_head, (query_stack, key_stack))
    return jnp.transpose(stacked, (1, 0, 2))


def block_levels(key, dims, cuts, smallest, largest):
    loudness, own = 1.0, jax.random.fold_in(key, 6)
    for dim, blocks in cuts:
        steps = jnp.exp(jax.random.uniform(jax.random.fold_in(own, dim), (blocks,), jnp.float32, smallest / len(cuts), largest / len(cuts)))
        loudness = loudness * jnp.repeat(steps, dims[dim] // blocks).reshape([-1 if axis == dim else 1 for axis in range(len(dims))])
    return loudness


def scatter_about(stream_key, shape, deviation, bound, pieces=(), held_as=jnp.bfloat16):
    drawn = jax.random.normal(stream_key, shape, jnp.float32) * deviation
    if len(pieces) > 0:
        drawn = block_levels(stream_key, shape, pieces, -0.22, 0.18) * drawn
    return jnp.clip(drawn, min=-bound, max=bound).astype(held_as)


def setup_inputs(seed: int = 0) -> dict:
    keys = jax.random.split(jax.random.key(seed), 11)
    layer_input = scatter_about(keys[0], (TOKENS, D), 0.05, 0.29882812, ((0, 16), (1, 16)))
    query_heads = draw_query_heads(jax.random.fold_in(keys[10], 71), 0)
    key_heads = draw_key_heads(jax.random.fold_in(keys[10], 71), 0)
    value_heads = scatter_about(keys[3], (TOKENS, HEADS * 2 * HALF), 1.0, 6.0, ((0, 16), (1, 16)))
    map_one_out = scatter_about(keys[4], (TOKENS, HEADS * 2 * HALF), 0.5, 3.0, ((0, 16), (1, 16)))
    map_two_out = scatter_about(keys[5], (TOKENS, HEADS * 2 * HALF), 0.5, 3.0, ((0, 16), (1, 16)))
    grad_out = scatter_about(keys[6], (TOKENS, HEADS * 2 * HALF), 1.0, 6.0, ((0, 16), (1, 16)))
    saved_lse = draw_saved_lse(jax.random.fold_in(keys[10], 71), 0)
    lambdas = jnp.clip(0.2 + 0.6 * jax.random.uniform(keys[8], (HEADS,), jnp.float32) ** block_levels(keys[8], (HEADS,), ((0, 16),), -0.2, 0.2), 0.2, 0.8)
    block_order = draw_block_order(jax.random.fold_in(keys[10], 71), 0)
    return {"layer_input": layer_input, "query_heads": query_heads, "key_heads": key_heads, "value_heads": value_heads, "map_one_out": map_one_out, "map_two_out": map_two_out, "grad_out": grad_out, "saved_lse": saved_lse, "lambdas": lambdas, "block_order": block_order}


score_scale = 0.08838834764831845


def reference(layer_input, query_heads, key_heads, value_heads, map_one_out, map_two_out, grad_out, saved_lse, lambdas, block_order):
    row_index = jnp.arange(TOKENS, dtype=jnp.int32)
    positions = block_order[row_index // TOK_DEV] * TOK_DEV + row_index % TOK_DEV
    visible = positions[None, :] <= positions[:, None]

    def to_heads(array):
        return jnp.transpose(array.reshape(TOKENS, HEADS, 2 * HALF), (1, 0, 2))

    def one_head(head_items):
        queries, key_rows, value_rows, out_one, out_two, grad_rows, lse_one, lse_two, lam_value = head_items
        score_one = jnp.dot(queries[:, :HALF], key_rows[:, :HALF].T, preferred_element_type=jnp.float32) * score_scale
        score_two = jnp.dot(queries[:, HALF:], key_rows[:, HALF:].T, preferred_element_type=jnp.float32) * score_scale
        probs_one = jnp.exp(jnp.where(visible, score_one - lse_one[:, None], -1e30))
        probs_two = jnp.exp(jnp.where(visible, score_two - lse_two[:, None], -1e30))
        upstream = jnp.dot(grad_rows, value_rows.T, preferred_element_type=jnp.float32)
        delta_one = jnp.sum(grad_rows.astype(jnp.float32) * out_one.astype(jnp.float32), axis=1)
        delta_two = -lam_value * jnp.sum(grad_rows.astype(jnp.float32) * out_two.astype(jnp.float32), axis=1)
        slope_one = (probs_one * (upstream - delta_one[:, None])).astype(jnp.bfloat16)
        slope_two = (probs_two * (-lam_value * upstream - delta_two[:, None])).astype(jnp.bfloat16)
        mixture = (probs_one - lam_value * probs_two).astype(jnp.bfloat16)
        grad_v = jnp.dot(mixture.T, grad_rows, preferred_element_type=jnp.float32).astype(jnp.bfloat16)
        grad_q = jnp.concatenate([
            jnp.dot(slope_one, key_rows[:, :HALF], preferred_element_type=jnp.float32),
            jnp.dot(slope_two, key_rows[:, HALF:], preferred_element_type=jnp.float32)], axis=1) * score_scale
        grad_k = jnp.concatenate([
            jnp.dot(slope_one.T, queries[:, :HALF], preferred_element_type=jnp.float32),
            jnp.dot(slope_two.T, queries[:, HALF:], preferred_element_type=jnp.float32)], axis=1) * score_scale
        return grad_q.astype(jnp.bfloat16), grad_k.astype(jnp.bfloat16), grad_v

    head_q, head_k, head_v = lax.map(one_head, (to_heads(query_heads), to_heads(key_heads), to_heads(value_heads), to_heads(map_one_out), to_heads(map_two_out), to_heads(grad_out), saved_lse[0], saved_lse[1], lambdas))

    def from_heads(array):
        return jnp.transpose(array, (1, 0, 2)).reshape(TOKENS, HEADS * 2 * HALF)

    grad_query = from_heads(head_q)
    grad_key = from_heads(head_k)
    grad_value = from_heads(head_v)
    weight_grad = jnp.stack([jnp.dot(layer_input.T, grad_block, preferred_element_type=jnp.float32) for grad_block in (grad_query, grad_key, grad_value)])
    return grad_query, grad_key, grad_value, weight_grad
```

```python
import functools
import math

import jax
import jax.numpy as jnp
from jax import lax
from jax.experimental import pallas as pl
from jax.experimental.pallas import tpu as pltpu
from jax.sharding import PartitionSpec as P

HALF = 128
WIDE = 256
LEN = 320
PAIR = 640
ALL = 1280
SCALE = 0.08838834764831845
LOG2E = 1.4426950408889634
F32 = jnp.float32
BF16 = jnp.bfloat16
MESH = pl.DeviceIdType.MESH

NN = (((1,), (0,)), ((), ()))
NT = (((1,), (1,)), ((), ()))


def dot(a, b, dims=NN):
    return lax.dot_general(a, b, dims, preferred_element_type=F32)


def kernel(
    x_ref, q_ref, k_ref, v_ref, o1_ref, o2_ref, g_ref, lse_ref, lam_ref, order_ref,
    dq_out, dk_out, dv_out, w_out,
    qb, gb, st, stp, kb, vb, kt, dkv, dqt,
    dqs, dqr, sib_s, sib_r, par_s, par_r, gw, lb, lt, ws, wr,
    send, recv, zsend, zrecv, lsend, lrecv, wsend, wrecv,
):
    c = lax.axis_index("ctx")
    h = lax.axis_index("head")
    yl, x, k = c // 8, (c // 2) % 4, c % 2
    yh, z = h // 8, h % 8

    def dev(yl_, x_, k_, yh_, z_):
        return ((yl_ * 4 + x_) * 2 + k_, yh_ * 8 + z_)

    def xdev(d):
        return dev(yl, (x + d) % 4, k, yh, z)

    def zdev(d):
        return dev(yl, x, k, yh, (z + d) % 8)

    sib = dev(yl, x, 1 - k, yh, z)
    par = dev(1 - yl, x, k, yh, z)

    barrier = pltpu.get_barrier_semaphore()
    partners = [xdev(1), xdev(2), xdev(3), zdev(1), zdev(7)]
    for a in range(2):
        for b in range(2):
            for e in range(2):
                if a + b + e > 0:
                    partners.append(dev((yl + a) % 2, x, (k + b) % 2, (yh + e) % 2, z))
    for p in partners:
        pl.semaphore_signal(barrier, inc=1, device_id=p, device_id_type=MESH)
    pl.semaphore_wait(barrier, len(partners))

    used = [0]

    def remote(src, dst, to):
        i = used[0]
        used[0] += 1
        return pltpu.make_async_remote_copy(
            src_ref=src, dst_ref=dst, send_sem=send.at[i], recv_sem=recv.at[i],
            device_id=to, device_id_type=MESH,
        )

    pending = []

    def go(cp):
        cp.start()
        pending.append(cp)
        return cp

    t_own = yl * 2 + k
    holder = k == z % 2
    home = yh == yl

    def l_copy(e):
        return pltpu.make_async_remote_copy(
            src_ref=x_ref, dst_ref=lb.at[t_own], send_sem=lsend.at[e], recv_sem=lrecv.at[t_own],
            device_id=dev(yh, x, z % 2, (yh + e) % 2, z), device_id_type=MESH,
        )

    mine = jnp.logical_and(holder, home)
    l_local = pltpu.make_async_copy(x_ref, lb.at[t_own], lrecv.at[t_own])

    @pl.when(mine)
    def _():
        l_local.start()

    @pl.when(jnp.logical_not(mine))
    def _():
        l_copy(0).start()

    l_copy(1).start()

    gq = [go(remote(q_ref, qb.at[s], xdev(d))) for s, d in ((1, 1), (2, 3))]
    gg = [go(remote(g_ref, gb.at[s], xdev(d))) for s, d in ((1, 1), (2, 3))]
    gk = [go(remote(k_ref, kb.at[1], sib)), go(remote(k_ref, kb.at[2], par))]
    gv = [go(remote(v_ref, vb.at[1], sib)), go(remote(v_ref, vb.at[2], par))]
    gq.append(go(remote(q_ref, qb.at[3], xdev(2))))
    gg.append(go(remote(g_ref, gb.at[3], xdev(2))))

    gf = g_ref[...].astype(F32)
    ones = jnp.ones((16, WIDE), BF16)

    def row_sums(o_ref):
        prod = gf * o_ref[...].astype(F32)
        hi = prod.astype(BF16)
        lo = (prod - hi.astype(F32)).astype(BF16)
        return (dot(ones, hi, NT) + dot(ones, lo, NT))[0:1]

    lam = jnp.full((1, LEN), lam_ref[0], F32)
    st[0, 0:1, :] = lse_ref[0] * LOG2E
    st[0, 1:2, :] = lse_ref[1] * LOG2E - jnp.log(lam) * LOG2E
    st[0, 2:3, :] = row_sums(o1_ref)
    st[0, 3:4, :] = row_sums(o2_ref)
    st[0, 4:8, :] = jnp.zeros((4, LEN), F32)
    gs = [go(remote(st.at[0], st.at[s], xdev(d))) for s, d in ((1, 1), (2, 3), (3, 2))]

    qb[0] = q_ref[...]
    gb[0] = g_ref[...]
    kb[0] = k_ref[...]
    vb[0] = v_ref[...]

    eye = (
        lax.broadcasted_iota(jnp.int32, (LEN, LEN), 0)
        == lax.broadcasted_iota(jnp.int32, (LEN, LEN), 1)
    ).astype(F32).astype(BF16)
    eye_wide = eye[0:WIDE, 0:WIDE]

    def transpose_keys(j):
        kt[j] = dot(eye_wide, kb[j], NT).astype(BF16)

    transpose_keys(0)

    def z_copy(src_z, half, way, event):
        rows = pl.ds(half * 160, 160)
        ref = lt.at[(src_z % 8) // 2, rows]
        return pltpu.make_async_remote_copy(
            src_ref=ref, dst_ref=ref,
            send_sem=zsend.at[way, event, half], recv_sem=zrecv.at[way, event, half],
            device_id=zdev(1 if way == 0 else 7), device_id_type=MESH,
        )

    @pl.when(holder)
    def _():
        for t in range(4):
            pltpu.make_async_copy(x_ref, lb.at[t], lrecv.at[t]).wait()
        lt[z // 2] = dot(eye, lb[...].reshape(ALL, LEN), NT).astype(BF16)
        for half in range(2):
            for way in range(2):
                z_copy(z, half, way, 0).start()

    def z_wait(event, half, way):
        z_copy(z, half, way, event).wait_recv()

    def arrived(way, far):
        return z - far + 8 if way == 0 else z + far

    def relay_near(half):
        @pl.when(jnp.logical_not(holder))
        def _():
            for way in range(2):
                z_wait(0, half, way)
                z_copy(arrived(way, 1), half, way, 0).start()

    def relay_mid(half):
        @pl.when(holder)
        def _():
            for way in range(2):
                z_wait(0, half, way)
                z_copy(arrived(way, 2), half, way, 1).start()

    def relay_far(half):
        @pl.when(jnp.logical_not(holder))
        def _():
            for way in range(2):
                z_wait(1, half, way)
                if way == half:
                    z_copy(arrived(way, 3), half, way, 1).start()

    def finish_z():
        @pl.when(holder)
        def _():
            for way in range(2):
                z_wait(1, way, way)

    def block(yl_, x_, k_):
        return order_ref[(yl_ * 4 + x_) * 2 + k_]

    q_pos = [block(yl, (x + d) % 4, k) for d in (0, 3, 1, 2)]
    first = lax.broadcasted_iota(jnp.int32, (1, PAIR), 1) < LEN

    def key_pos(j):
        return block((yl + j // 2) % 2, x, (k + j % 2) % 2)

    def attend(p, j, diagonal, fresh_keys, fresh_queries):
        rows = slice(p * PAIR, (p + 1) * PAIR)
        qs = qb[2 * p : 2 * p + 2].reshape(PAIR, WIDE)
        grads = gb[2 * p : 2 * p + 2].reshape(PAIR, WIDE)
        keys = kb[j]
        pos = key_pos(j)
        hide = jnp.where(
            first,
            jnp.where(pos > q_pos[2 * p], 1e30, 0.0),
            jnp.where(pos > q_pos[2 * p + 1], 1e30, 0.0),
        )
        stats = stp[p]
        up = dot(vb[j], grads, NT)
        p1 = jnp.exp2(dot(keys[:, :HALF], qs[:, :HALF], NT) * (SCALE * LOG2E) - (stats[0:1] + hide))
        p2 = jnp.exp2(dot(keys[:, HALF:], qs[:, HALF:], NT) * (SCALE * LOG2E) - (stats[1:2] + hide))
        if diagonal:
            key_row = lax.broadcasted_iota(jnp.int32, (LEN, PAIR), 0)
            query_col = lax.broadcasted_iota(jnp.int32, (LEN, PAIR), 1)
            seen = key_row <= query_col
            p1 = jnp.where(seen, p1, 0.0)
            p2 = jnp.where(seen, p2, 0.0)
        s1 = (p1 * (up - stats[2:3])).astype(BF16)
        s2 = (p2 * (up - stats[3:4])).astype(BF16)
        mix = (p1 - p2).astype(BF16)
        dk1 = dot(s1, qs[:, :HALF])
        dk2 = dot(s2, qs[:, HALF:])
        dv = dot(mix, grads)
        if fresh_keys:
            dkv[j, :, 0:HALF] = dk1
            dkv[j, :, HALF:WIDE] = dk2
            dkv[j, :, WIDE:] = dv
        else:
            dkv[j, :, 0:HALF] += dk1
            dkv[j, :, HALF:WIDE] += dk2
            dkv[j, :, WIDE:] += dv
        dq1 = dot(kt[j, 0:HALF, :], s1)
        dq2 = dot(kt[j, HALF:WIDE, :], s2)
        if fresh_queries:
            dqt[p, 0:HALF] = dq1
            dqt[p, HALF:WIDE] = dq2
        else:
            dqt[p, 0:HALF] += dq1
            dqt[p, HALF:WIDE] += dq2

    def finish_dq(p):
        return dqt[p].T

    def signed(t):
        sign = jnp.where(lax.broadcasted_iota(jnp.int32, (1, WIDE), 1) < HALF, SCALE, -SCALE)
        return t * sign

    gq[0].wait_recv()
    gg[0].wait_recv()
    gs[0].wait_recv()
    stp[0] = jnp.concatenate([st[0], st[1]], axis=1)
    attend(0, 0, True, True, True)
    gk[0].wait_recv()
    gv[0].wait_recv()
    transpose_keys(1)
    gk[1].wait_recv()
    rk = go(remote(kb.at[2], kb.at[3], sib))
    gv[1].wait_recv()
    rv = go(remote(vb.at[2], vb.at[3], sib))
    transpose_keys(2)
    rk.wait_recv()
    rv.wait_recv()
    transpose_keys(3)

    def early(j, carry):
        attend(0, j, False, True, False)
        return carry

    lax.fori_loop(1, 4, early, 0)
    relay_near(0)

    dq_a = finish_dq(0)
    dqs[0] = dq_a[LEN:PAIR].astype(BF16)
    sq = [go(remote(dqs.at[0], dqr.at[0], xdev(3)))]

    for i in (1, 2):
        gq[i].wait_recv()
        gg[i].wait_recv()
        gs[i].wait_recv()
    stp[1] = jnp.concatenate([st[2], st[3]], axis=1)
    dqt[1] = jnp.zeros_like(dqt[1])

    def late(i, carry):
        attend(1, 3 - i, False, False, False)
        return carry

    lax.fori_loop(0, 2, late, 0)
    sib_s[0] = dkv[3].astype(BF16)
    b0 = go(remote(sib_s.at[0], sib_r.at[0], sib))
    relay_near(1)
    b0.wait_recv()
    par_s[...] = (dkv[2] + sib_r[0].astype(F32)).astype(BF16)
    b1 = go(remote(par_s, par_r, par))
    lax.fori_loop(2, 4, late, 0)
    dq_b = finish_dq(1)
    dqs[1] = dq_b[0:LEN].astype(BF16)
    dqs[2] = dq_b[LEN:PAIR].astype(BF16)
    sq.append(go(remote(dqs.at[1], dqr.at[1], xdev(1))))
    sq.append(go(remote(dqs.at[2], dqr.at[2], xdev(2))))
    sib_s[1] = dkv[1].astype(BF16)
    b2 = go(remote(sib_s.at[1], sib_r.at[1], sib))
    relay_mid(0)

    own_rows = pl.ds(pl.multiple_of(t_own * LEN, LEN), LEN)

    def share(i, value, out):
        out[...] = value
        ref = gw.at[i, own_rows]
        ref[...] = value
        return [go(remote(ref, ref, sib)), go(remote(ref, ref, par))]

    par_rows = pl.ds(pl.multiple_of(((1 - yl) * 2 + k) * LEN, LEN), LEN)

    def pass_on(i, copies):
        copies[1].wait_recv()
        ref = gw.at[i, par_rows]
        copies.append(go(remote(ref, ref, sib)))

    for cp in sq:
        cp.wait_recv()
    total = dqt[0].T[0:LEN]
    for i in range(3):
        total = total + dqr[i].astype(F32)
    c0 = share(0, signed(total).astype(BF16), dq_out)

    b1.wait_recv()
    b2.wait_recv()
    total = dkv[0] + sib_r[1].astype(F32) + par_r[...].astype(F32)
    c1 = share(1, signed(total[:, 0:WIDE]).astype(BF16), dk_out)
    c2 = share(2, total[:, WIDE:].astype(BF16), dv_out)
    relay_mid(1)
    pass_on(0, c0)
    relay_far(0)
    pass_on(1, c1)
    relay_far(1)
    pass_on(2, c2)
    finish_z()
    for cps in (c0, c1, c2):
        cps[0].wait_recv()
        cps[2].wait_recv()

    def w_copy(i, r):
        return pltpu.make_async_remote_copy(
            src_ref=ws.at[r - 1, i], dst_ref=wr.at[r - 1, i],
            send_sem=wsend.at[r - 1, i], recv_sem=wrecv.at[r - 1, i],
            device_id=xdev(r), device_id_type=MESH,
        )

    for i in range(3):
        def part(r, carry):
            ws[r - 1, i] = dot(lt[(x + r) % 4], gw[i]).astype(BF16)
            w_copy(i, r).start()
            return carry

        lax.fori_loop(1, 4, part, 0)
    for i in range(3):
        w_out[i] = dot(lt[x], gw[i])
    for i in range(3):
        for r in range(1, 4):
            w_copy(i, r).wait_recv()
        w_out[i] += wr[0, i].astype(F32) + wr[1, i].astype(F32) + wr[2, i].astype(F32)

    for cp in pending:
        cp.wait_send()

    @pl.when(jnp.logical_not(mine))
    def _():
        l_copy(0).wait_send()

    l_copy(1).wait_send()
    for half in range(2):
        for way in range(2):
            z_copy(z, half, way, 0).wait_send()

            @pl.when(jnp.logical_or(holder, way == half))
            def _():
                z_copy(z, half, way, 1).wait_send()

    for i in range(3):
        for r in range(1, 4):
            w_copy(i, r).wait_send()


def body(*args):
    vmem = pl.BlockSpec(memory_space=pltpu.VMEM)
    smem = pl.BlockSpec(memory_space=pltpu.SMEM)
    grad = jax.ShapeDtypeStruct((LEN, WIDE), BF16)
    dma = pltpu.SemaphoreType.DMA
    return pl.pallas_call(
        kernel,
        out_shape=(grad, grad, grad, jax.ShapeDtypeStruct((3, LEN, WIDE), F32)),
        in_specs=[vmem] * 8 + [smem] * 2,
        out_specs=(vmem,) * 4,
        scratch_shapes=[
            pltpu.VMEM((4, LEN, WIDE), BF16),
            pltpu.VMEM((4, LEN, WIDE), BF16),
            pltpu.VMEM((4, 8, LEN), F32),
            pltpu.VMEM((2, 8, PAIR), F32),
            pltpu.VMEM((4, LEN, WIDE), BF16),
            pltpu.VMEM((4, LEN, WIDE), BF16),
            pltpu.VMEM((4, WIDE, LEN), BF16),
            pltpu.VMEM((4, LEN, 2 * WIDE), F32),
            pltpu.VMEM((2, WIDE, PAIR), F32),
            pltpu.VMEM((3, LEN, WIDE), BF16),
            pltpu.VMEM((3, LEN, WIDE), BF16),
            pltpu.VMEM((2, LEN, 2 * WIDE), BF16),
            pltpu.VMEM((2, LEN, 2 * WIDE), BF16),
            pltpu.VMEM((LEN, 2 * WIDE), BF16),
            pltpu.VMEM((LEN, 2 * WIDE), BF16),
            pltpu.VMEM((3, ALL, WIDE), BF16),
            pltpu.VMEM((4, LEN, LEN), BF16),
            pltpu.VMEM((4, LEN, ALL), BF16),
            pltpu.VMEM((3, 3, LEN, WIDE), BF16),
            pltpu.VMEM((3, 3, LEN, WIDE), BF16),
            dma((32,)),
            dma((32,)),
            dma((2, 2, 2)),
            dma((2, 2, 2)),
            dma((2,)),
            dma((4,)),
            dma((3, 3)),
            dma((3, 3)),
        ],
        compiler_params=pltpu.CompilerParams(
            collective_id=0, has_side_effects=True, vmem_limit_bytes=56 * 2**20
        ),
        name="diff_attention_backward",
    )(*args)


def solution(mesh):
    in_specs = (P("ctx", "head"),) * 7 + (P(None, "head", "ctx"), P("head"), P())
    out_specs = (P("ctx", "head"), P("ctx", "head"), P("ctx", "head"), P(None, "ctx", "head"))
    return jax.shard_map(body, mesh=mesh, in_specs=in_specs, out_specs=out_specs, check_vma=False)
```

```python
import functools
import math

import jax
import jax.numpy as jnp
from jax import lax
from jax.experimental import pallas as pl
from jax.experimental.pallas import tpu as pltpu
from jax.sharding import PartitionSpec as P

HALF = 128
WIDE = 256
LEN = 320
PAIR = 640
TILE = 256
ALL = 1280
SCALE = 0.08838834764831845
LOG2E = 1.4426950408889634
F32 = jnp.float32
BF16 = jnp.bfloat16
MESH = pl.DeviceIdType.MESH

NN = (((1,), (0,)), ((), ()))
NT = (((1,), (1,)), ((), ()))


def dot(a, b, dims=NN):
    return lax.dot_general(a, b, dims, preferred_element_type=F32)


def kernel(
    x_ref, q_ref, k_ref, v_ref, o1_ref, o2_ref, g_ref, lse_ref, lam_ref, order_ref,
    dq_out, dk_out, dv_out, w_out,
    qb, gb, st, stp, kb, vb, kt, dkv, dqt, dqf,
    dqs, dqr, sib_s, sib_r, par_s, par_r, gw, xp, lb, tb, zb, sb, pp, hr, ws, wr,
    send, recv, zsend, zrecv, dsend, drecv, tsend, trecv, lsend, lrecv, hsend, hrecv, wsend, wrecv,
):
    c = lax.axis_index("ctx")
    h = lax.axis_index("head")
    yl, x, k = c // 8, (c // 2) % 4, c % 2
    yh, z = h // 8, h % 8

    def dev(yl_, x_, k_, yh_, z_):
        return ((yl_ * 4 + x_) * 2 + k_, yh_ * 8 + z_)

    def xdev(d):
        return dev(yl, (x + d) % 4, k, yh, z)

    def zdev(d):
        return dev(yl, x, k, yh, (z + d) % 8)

    sib = dev(yl, x, 1 - k, yh, z)
    par = dev(1 - yl, x, k, yh, z)

    barrier = pltpu.get_barrier_semaphore()
    partners = [xdev(1), xdev(2), xdev(3), zdev(1), zdev(7)]
    for a in range(2):
        for b in range(2):
            for e in range(2):
                if a + b + e > 0:
                    partners.append(dev((yl + a) % 2, x, (k + b) % 2, (yh + e) % 2, z))
    for p in partners:
        pl.semaphore_signal(barrier, inc=1, device_id=p, device_id_type=MESH)
    xp[...] = jnp.concatenate([x_ref[0 : LEN // 2], x_ref[LEN // 2 : LEN]], axis=1)
    pl.semaphore_wait(barrier, len(partners))

    used = [0]

    def remote(src, dst, to):
        i = used[0]
        used[0] += 1
        return pltpu.make_async_remote_copy(
            src_ref=src, dst_ref=dst, send_sem=send.at[i], recv_sem=recv.at[i],
            device_id=to, device_id_type=MESH,
        )

    pending = []

    def go(cp):
        cp.start()
        pending.append(cp)
        return cp

    def slot(ref, j):
        return ref.at[pl.ds(j * LEN, LEN)]

    def l_copy(e):
        return pltpu.make_async_remote_copy(
            src_ref=xp, dst_ref=lb.at[k], send_sem=lsend.at[e], recv_sem=lrecv.at[k],
            device_id=dev(yh, x, yl, (yh + e) % 2, z), device_id_type=MESH,
        )

    mine = jnp.logical_and(yh == yl, k == yl)
    l_local = pltpu.make_async_copy(xp, lb.at[k], lrecv.at[k])

    @pl.when(mine)
    def _():
        l_local.start()

    l_copy(1).start()

    @pl.when(jnp.logical_not(mine))
    def _():
        l_copy(0).start()

    q1 = go(remote(q_ref, slot(qb, 1), xdev(1)))
    g2 = go(remote(g_ref, slot(gb, 2), xdev(3)))
    g1 = go(remote(g_ref, slot(gb, 1), xdev(1)))
    q2 = go(remote(q_ref, slot(qb, 2), xdev(3)))
    ks = go(remote(k_ref, slot(kb, 1), sib))
    vs = go(remote(v_ref, slot(vb, 1), sib))

    gf = g_ref[...].astype(F32)
    ones = jnp.ones((16, WIDE), BF16)

    def row_sums(o_ref):
        prod = gf * o_ref[...].astype(F32)
        hi = prod.astype(BF16)
        lo = (prod - hi.astype(F32)).astype(BF16)
        return (dot(ones, hi, NT) + dot(ones, lo, NT))[0:1]

    def position(yl_, x_, k_):
        return order_ref[(yl_ * 4 + x_) * 2 + k_].astype(F32)

    lam = jnp.full((1, LEN), lam_ref[0], F32)
    st[0, 0:1, :] = lse_ref[0] * LOG2E
    st[0, 1:2, :] = lse_ref[1] * LOG2E - jnp.log(lam) * LOG2E
    st[0, 2:3, :] = row_sums(o1_ref)
    st[0, 3:4, :] = row_sums(o2_ref)
    st[0, 4:5, :] = jnp.full((1, LEN), position(yl, x, k), F32)
    st[0, 5:8, :] = jnp.zeros((3, LEN), F32)
    gs = [go(remote(st.at[0], st.at[s], xdev(d))) for s, d in ((1, 1), (2, 3), (3, 2))]

    kp = go(remote(k_ref, slot(kb, 2), par))
    vp = go(remote(v_ref, slot(vb, 2), par))
    qb[0:LEN] = q_ref[...]
    gb[0:LEN] = g_ref[...]
    kb[0:LEN] = k_ref[...]
    vb[0:LEN] = v_ref[...]

    eye = (
        lax.broadcasted_iota(jnp.int32, (LEN, LEN), 0)
        == lax.broadcasted_iota(jnp.int32, (LEN, LEN), 1)
    ).astype(F32).astype(BF16)
    eye_wide = eye[0:WIDE, 0:WIDE]

    match = z % 2 == k
    soon = jnp.where(yh == yl, yl, 1 - yl)
    later = 1 - soon

    def z_copy(src, dst, pair, way):
        return pltpu.make_async_remote_copy(
            src_ref=zb.at[src, pair], dst_ref=zb.at[dst, pair],
            send_sem=zsend.at[dst, pair], recv_sem=zrecv.at[dst, pair],
            device_id=zdev(1 if way == 0 else 7), device_id_type=MESH,
        )

    def d_copy(i):
        return pltpu.make_async_remote_copy(
            src_ref=zb.at[i], dst_ref=sb.at[i], send_sem=dsend.at[i], recv_sem=drecv.at[i],
            device_id=sib, device_id_type=MESH,
        )

    def hand_over(places, far):
        @pl.when(match if far % 2 else jnp.logical_not(match))
        def _():
            for i in places:
                d_copy(i).start()

    def t_copy(pair):
        rows = pl.ds(pl.multiple_of((1 - k) * (LEN // 2), 32), LEN // 2)
        return pltpu.make_async_remote_copy(
            src_ref=tb.at[rows], dst_ref=zb.at[7, pair], send_sem=tsend.at[0],
            recv_sem=trecv.at[0], device_id=sib, device_id_type=MESH,
        )

    def z_turn():
        for b in range(2):
            pltpu.make_async_copy(xp, lb.at[b], lrecv.at[b]).wait()
        parts = [lb[b, :, i * LEN : (i + 1) * LEN] for b in range(2) for i in range(2)]
        tb[...] = dot(eye, jnp.concatenate(parts, axis=0), NT).astype(BF16)
        t_copy(k).start()
        zb[7, k] = tb[pl.ds(pl.multiple_of(k * (LEN // 2), 32), LEN // 2)]

    def z_begin(pair):
        @pl.when(pair == k)
        def _():
            z_turn()

        @pl.when(pair != k)
        def _():
            t_copy(1 - k).wait_recv()

        for way in range(2):
            z_copy(7, way, pair, way).start()

    def relay(far, pair):
        for way in range(2):
            place = 2 * (far - 1) + way
            z_copy(place, place, pair, way).wait_recv()
            if far < 3:
                z_copy(place, place + 2, pair, way).start()
            else:
                @pl.when(pair == way)
                def _():
                    z_copy(place, 6, pair, way).start()

    def finish_z():
        for way in range(2):
            z_copy(6, 6, way, way).wait_recv()
        hand_over((6,), 4)

    def ahead(f, *args):
        pl.when(yh == yl)(lambda: f(*args))

    def behind(f, *args):
        pl.when(yh != yl)(lambda: f(*args))

    def begin_later():
        z_begin(later)
        hand_over((7,), 0)

    def relay_later(far):
        relay(far, later)
        hand_over((2 * far - 2, 2 * far - 1), far)

    ahead(z_begin, soon)
    dkv[...] = jnp.zeros_like(dkv)
    dqt[...] = jnp.zeros_like(dqt)
    ks.wait_recv()
    kt[0] = dot(eye_wide, kb[0:PAIR], NT).astype(BF16)
    q1.wait_recv()
    q3 = go(remote(slot(qb, 1), slot(qb, 3), xdev(1)))
    g2.wait_recv()
    g3 = go(remote(slot(gb, 2), slot(gb, 3), xdev(3)))

    def attend(m, t):
        keys_at = slice(m * PAIR, (m + 1) * PAIR)
        tile = pl.ds(pl.multiple_of(t * TILE, TILE), TILE)
        qs, grads, stats = qb[tile], gb[tile], stp[t]
        keys = kb[keys_at]
        up = dot(vb[keys_at], grads, NT)
        score1 = dot(keys[:, :HALF], qs[:, :HALF], NT)
        score2 = dot(keys[:, HALF:], qs[:, HALF:], NT)
        s1, s2, mix = [], [], []
        for b in range(2):
            part = slice(b * LEN, (b + 1) * LEN)
            key_pos = position((yl + m) % 2, x, (k + b) % 2)
            hide = jnp.where(stats[4:5] < key_pos, 1e30, 0.0)
            p1 = jnp.exp2(score1[part] * (SCALE * LOG2E) - (stats[0:1] + hide))
            p2 = jnp.exp2(score2[part] * (SCALE * LOG2E) - (stats[1:2] + hide))
            if m == 0 and b == 0:
                key_row = lax.broadcasted_iota(jnp.int32, (LEN, TILE), 0)
                query_col = lax.broadcasted_iota(jnp.int32, (LEN, TILE), 1) + t * TILE
                p1 = jnp.where(key_row <= query_col, p1, 0.0)
                p2 = jnp.where(key_row <= query_col, p2, 0.0)
            s1.append((p1 * (up[part] - stats[2:3])).astype(BF16))
            s2.append((p2 * (up[part] - stats[3:4])).astype(BF16))
            mix.append((p1 - p2).astype(BF16))
        s1, s2, mix = (jnp.concatenate(a, axis=0) for a in (s1, s2, mix))
        dkv[keys_at, 0:HALF] += dot(s1, qs[:, :HALF])
        dkv[keys_at, HALF:WIDE] += dot(s2, qs[:, HALF:])
        dkv[keys_at, WIDE:] += dot(mix, grads)
        dqt[t, 0:HALF] += dot(kt[m, 0:HALF, :], s1)
        dqt[t, HALF:WIDE] += dot(kt[m, HALF:WIDE, :], s2)

    def sweep(m, low, high):
        def step(t, carry):
            attend(m, t)
            return carry

        lax.fori_loop(low, high, step, 0)

    def signed(t):
        sign = jnp.where(lax.broadcasted_iota(jnp.int32, (1, WIDE), 1) < HALF, SCALE, -SCALE)
        return t * sign

    def both_cores(j, i):
        sib_s[i] = dkv[j * LEN : (j + 1) * LEN].astype(BF16)
        return go(remote(sib_s.at[i], sib_r.at[i], sib))

    g1.wait_recv()
    gs[0].wait_recv()
    vs.wait_recv()
    behind(z_begin, soon)
    q2.wait_recv()
    gs[1].wait_recv()
    near = jnp.concatenate([st[0], st[1], st[2]], axis=1)
    for t in range(3):
        stp[t] = near[:, t * TILE : (t + 1) * TILE]
    sweep(0, 0, 2)
    ahead(relay, 1, soon)
    sweep(0, 2, 3)
    kp.wait_recv()
    rk = go(remote(slot(kb, 2), slot(kb, 3), sib))
    vp.wait_recv()
    rv = go(remote(slot(vb, 2), slot(vb, 3), sib))
    ahead(begin_later)
    behind(relay, 1, soon)
    rk.wait_recv()
    rv.wait_recv()
    kt[1] = dot(eye_wide, kb[PAIR:ALL], NT).astype(BF16)
    sweep(1, 0, 3)

    def turn_dq(t):
        dqf[t * TILE : (t + 1) * TILE] = dqt[t].T

    def send_dq(s, d):
        dqs[s - 1] = dqf[s * LEN : (s + 1) * LEN].astype(BF16)
        return go(remote(dqs.at[s - 1], dqr.at[s - 1], xdev(d)))

    for t in range(3):
        turn_dq(t)
    sq = [send_dq(1, 3)]
    ahead(relay, 2, soon)
    behind(begin_later)

    q3.wait_recv()
    g3.wait_recv()
    gs[2].wait_recv()
    far = jnp.concatenate([st[2], st[3]], axis=1)
    for t in (3, 4):
        stp[t] = far[:, t * TILE - 2 * LEN : (t + 1) * TILE - 2 * LEN]
    sweep(1, 3, 5)
    b0 = both_cores(3, 0)
    sweep(0, 3, 5)
    ahead(relay_later, 1)
    b1 = both_cores(1, 1)
    turn_dq(3)
    turn_dq(4)
    sq.append(send_dq(3, 2))
    sq.append(send_dq(2, 1))

    def rows_of(yl_, k_):
        return pl.ds(pl.multiple_of((yl_ * 2 + k_) * LEN, LEN), LEN)

    columns = (None, slice(0, WIDE), slice(WIDE, 2 * WIDE))

    def chip_sum(i, b):
        return dkv[2 * b * LEN : (2 * b + 1) * LEN, columns[i]] + sib_r[1 - b, :, columns[i]].astype(F32)

    def exchange(i, b):
        par_s[b, i - 1] = chip_sum(i, b).astype(BF16)
        return go(remote(par_s.at[b, i - 1], par_r.at[1 - b, i - 1], par))

    def total(i, b, came):
        came.wait_recv()
        value = chip_sum(i, b) + par_r[b, i - 1].astype(F32)
        value = (signed(value) if i == 1 else value).astype(BF16)
        ref = gw.at[i, rows_of(yl if b == 0 else 1 - yl, k)]
        ref[...] = value
        if b == 0:
            (dk_out if i == 1 else dv_out)[...] = value
        return go(remote(ref, ref, sib))

    b0.wait_recv()
    e1 = exchange(1, 1)
    b1.wait_recv()
    e0 = exchange(1, 0)
    behind(relay, 2, soon)
    f1 = exchange(2, 1)
    ahead(relay, 3, soon)
    c_own = total(1, 0, e1)
    behind(relay_later, 1)
    for cp in sq:
        cp.wait_recv()
    value = dqf[0:LEN]
    for i in range(3):
        value = value + dqr[i].astype(F32)
    value = signed(value).astype(BF16)
    dq_out[...] = value
    ref = gw.at[0, rows_of(yl, k)]
    ref[...] = value
    q_par = go(remote(ref, ref, par))
    q_sib = go(remote(ref, ref, sib))
    ahead(relay_later, 2)
    c_par = total(1, 1, e0)
    f0 = exchange(2, 0)
    behind(relay, 3, soon)

    def h_copy(i, way):
        return pltpu.make_async_remote_copy(
            src_ref=ws.at[2, i, pl.ds(way * (LEN // 2), LEN // 2)], dst_ref=hr.at[way, i],
            send_sem=hsend.at[way, i], recv_sem=hrecv.at[way, i],
            device_id=xdev(1 if way == 0 else 3), device_id_type=MESH,
        )

    def w_copy(i, way):
        return pltpu.make_async_remote_copy(
            src_ref=ws.at[way, i], dst_ref=wr.at[way, i],
            send_sem=wsend.at[way, i], recv_sem=wrecv.at[way, i],
            device_id=xdev(1 if way == 0 else 3), device_id_type=MESH,
        )

    def place_of(r):
        ahead = (2 * ((x + r) % 4) + k - z + 8) % 8
        place = jnp.where(ahead == 0, 7, 6)
        for far, at in ((1, 1), (7, 0), (2, 3), (6, 2), (3, 5), (5, 4)):
            place = jnp.where(ahead == far, at, place)
        return place

    own_half = pl.ds(pl.multiple_of(k * (LEN // 2), 32), LEN // 2)
    other_half = pl.ds(pl.multiple_of((1 - k) * (LEN // 2), 32), LEN // 2)

    def project(i, r):
        p = place_of(r)
        chunk = [jnp.concatenate([ref[p, 0], ref[p, 1]], axis=1) for ref in (zb, sb)]
        part = dot(jnp.concatenate(chunk, axis=0), gw[i])
        if r == 2:
            ws[2, i, own_half] = part[: LEN // 2].astype(BF16)
            ws[2, i, other_half] = part[LEN // 2 :].astype(BF16)
            for way in range(2):
                h_copy(i, way).start()
        else:
            to = w_out.at[i] if r == 0 else pp.at[r // 2, i]
            to[own_half] = part[: LEN // 2]
            to[other_half] = part[LEN // 2 :]

    def forward(i):
        for way in range(2):
            rows = slice(way * (LEN // 2), (way + 1) * (LEN // 2))
            rest = slice((1 - way) * (LEN // 2), (2 - way) * (LEN // 2))
            ws[way, i, rest] = pp[way, i, rest].astype(BF16)
            h_copy(i, way).wait_recv()
            ws[way, i, rows] = (pp[way, i, rows] + hr[way, i].astype(F32)).astype(BF16)
            w_copy(i, way).start()

    c_own.wait_recv()
    c_par.wait_recv()
    q_par.wait_recv()
    ref = gw.at[0, rows_of(1 - yl, k)]
    q_far = go(remote(ref, ref, sib))
    ahead(relay_later, 3)
    behind(relay_later, 2)
    q_sib.wait_recv()
    q_far.wait_recv()
    c_own = total(2, 0, f1)
    ahead(finish_z)
    c_par = total(2, 1, f0)
    behind(relay_later, 3)
    behind(finish_z)
    for r in range(4):
        d_copy(place_of(r)).wait_recv()
    for r in (2, 1, 3):
        project(1, r)
    project(0, 2)
    forward(1)
    project(0, 1)
    project(0, 3)
    project(1, 0)
    c_own.wait_recv()
    c_par.wait_recv()
    project(2, 2)
    forward(0)
    project(2, 1)
    project(2, 3)
    project(0, 0)
    forward(2)
    project(2, 0)
    for i in (1, 0, 2):
        for way in range(2):
            w_copy(i, way).wait_recv()
        w_out[i] += wr[0, i].astype(F32) + wr[1, i].astype(F32)

    for cp in pending:
        cp.wait_send()

    @pl.when(jnp.logical_not(mine))
    def _():
        l_copy(0).wait_send()

    l_copy(1).wait_send()
    t_copy(k).wait_send()
    for place in range(6):
        for pair in range(2):
            z_copy(7, place, pair, 0).wait_send()
    for pair in range(2):
        z_copy(7, 6, pair, pair).wait_send()
    for far, places in ((0, (7,)), (1, (0, 1)), (2, (2, 3)), (3, (4, 5)), (4, (6,))):
        @pl.when(match if far % 2 else jnp.logical_not(match))
        def _():
            for i in places:
                d_copy(i).wait_send()

    for i in range(3):
        for way in range(2):
            h_copy(i, way).wait_send()
            w_copy(i, way).wait_send()


def tail(a, b, c, d, a_out, b_out, c_out, d_out, sems):
    copies = [
        pltpu.make_async_copy(src, dst, sems.at[i])
        for i, (src, dst) in enumerate(((d, d_out), (a, a_out), (b, b_out), (c, c_out)))
    ]
    for cp in copies:
        cp.start()
    for cp in copies:
        cp.wait()


def body(*args):
    vmem = pl.BlockSpec(memory_space=pltpu.VMEM)
    smem = pl.BlockSpec(memory_space=pltpu.SMEM)
    grad = jax.ShapeDtypeStruct((LEN, WIDE), BF16)
    dma = pltpu.SemaphoreType.DMA
    shapes = (grad, grad, grad, jax.ShapeDtypeStruct((3, LEN, WIDE), F32))
    results = pl.pallas_call(
        kernel,
        out_shape=shapes,
        in_specs=[vmem] * 8 + [smem] * 2,
        out_specs=(vmem,) * 4,
        scratch_shapes=[
            pltpu.VMEM((ALL, WIDE), BF16),
            pltpu.VMEM((ALL, WIDE), BF16),
            pltpu.VMEM((4, 8, LEN), F32),
            pltpu.VMEM((5, 8, TILE), F32),
            pltpu.VMEM((ALL, WIDE), BF16),
            pltpu.VMEM((ALL, WIDE), BF16),
            pltpu.VMEM((2, WIDE, PAIR), BF16),
            pltpu.VMEM((ALL, 2 * WIDE), F32),
            pltpu.VMEM((5, WIDE, TILE), F32),
            pltpu.VMEM((ALL, WIDE), F32),
            pltpu.VMEM((3, LEN, WIDE), BF16),
            pltpu.VMEM((3, LEN, WIDE), BF16),
            pltpu.VMEM((2, LEN, 2 * WIDE), BF16),
            pltpu.VMEM((2, LEN, 2 * WIDE), BF16),
            pltpu.VMEM((2, 2, LEN, WIDE), BF16),
            pltpu.VMEM((2, 2, LEN, WIDE), BF16),
            pltpu.VMEM((3, ALL, WIDE), BF16),
            pltpu.VMEM((LEN // 2, PAIR), BF16),
            pltpu.VMEM((2, LEN // 2, PAIR), BF16),
            pltpu.VMEM((LEN, PAIR), BF16),
            pltpu.VMEM((8, 2, LEN // 2, PAIR), BF16),
            pltpu.VMEM((8, 2, LEN // 2, PAIR), BF16),
            pltpu.VMEM((2, 3, LEN, WIDE), F32),
            pltpu.VMEM((2, 3, LEN // 2, WIDE), BF16),
            pltpu.VMEM((3, 3, LEN, WIDE), BF16),
            pltpu.VMEM((2, 3, LEN, WIDE), BF16),
            dma((32,)),
            dma((32,)),
            dma((7, 2)),
            dma((7, 2)),
            dma((8,)),
            dma((8,)),
            dma((1,)),
            dma((1,)),
            dma((2,)),
            dma((2,)),
            dma((2, 3)),
            dma((2, 3)),
            dma((2, 3)),
            dma((2, 3)),
        ],
        compiler_params=pltpu.CompilerParams(
            collective_id=0, has_side_effects=True, vmem_limit_bytes=56 * 2**20
        ),
        name="diff_attention_backward",
    )(*args)
    return pl.pallas_call(
        tail,
        out_shape=shapes,
        in_specs=[vmem] * 4,
        out_specs=(pl.BlockSpec(memory_space=pl.ANY),) * 4,
        scratch_shapes=[dma((4,))],
        name="write_results",
    )(*results)


def solution(mesh):
    in_specs = (P("ctx", "head"),) * 7 + (P(None, "head", "ctx"), P("head"), P())
    out_specs = (P("ctx", "head"), P("ctx", "head"), P("ctx", "head"), P(None, "ctx", "head"))
    return jax.shard_map(body, mesh=mesh, in_specs=in_specs, out_specs=out_specs, check_vma=False)
```

```python
import functools
import math

import jax
import jax.numpy as jnp
from jax import lax
from jax.experimental import pallas as pl
from jax.experimental.pallas import tpu as pltpu
from jax.sharding import PartitionSpec as P

HALF = 128
WIDE = 256
LEN = 320
PAIR = 640
TILE = 256
ALL = 1280
SCALE = 0.08838834764831845
LOG2E = 1.4426950408889634
F32 = jnp.float32
BF16 = jnp.bfloat16
MESH = pl.DeviceIdType.MESH

NN = (((1,), (0,)), ((), ()))
NT = (((1,), (1,)), ((), ()))


def dot(a, b, dims=NN):
    return lax.dot_general(a, b, dims, preferred_element_type=F32)


def kernel(
    x_ref, q_ref, k_ref, v_ref, o1_ref, o2_ref, g_ref, lse_ref, lam_ref, order_ref,
    dq_out, dk_out, dv_out, w_out,
    qb, gb, st, stp, kb, vb, kt, dkv, dqt, dqf,
    dqs, dqr, sib_s, sib_r, par_s, par_r, gw, xp, lb, tb, zb, sb, pp, hr, ws, wr,
    send, recv, zsend, zrecv, dsend, drecv, tsend, trecv, lsend, lrecv, hsend, hrecv, wsend, wrecv,
):
    c = lax.axis_index("ctx")
    h = lax.axis_index("head")
    yl, x, k = c // 8, (c // 2) % 4, c % 2
    yh, z = h // 8, h % 8

    def dev(yl_, x_, k_, yh_, z_):
        return ((yl_ * 4 + x_) * 2 + k_, yh_ * 8 + z_)

    def xdev(d):
        return dev(yl, (x + d) % 4, k, yh, z)

    def zdev(d):
        return dev(yl, x, k, yh, (z + d) % 8)

    sib = dev(yl, x, 1 - k, yh, z)
    par = dev(1 - yl, x, k, yh, z)

    barrier = pltpu.get_barrier_semaphore()
    partners = [xdev(1), xdev(2), xdev(3), zdev(1), zdev(7)]
    for a in range(2):
        for b in range(2):
            for e in range(2):
                if a + b + e > 0:
                    partners.append(dev((yl + a) % 2, x, (k + b) % 2, (yh + e) % 2, z))
    for p in partners:
        pl.semaphore_signal(barrier, inc=1, device_id=p, device_id_type=MESH)
    xp[...] = jnp.concatenate([x_ref[0 : LEN // 2], x_ref[LEN // 2 : LEN]], axis=1)
    pl.semaphore_wait(barrier, len(partners))

    used = [0]

    def remote(src, dst, to):
        i = used[0]
        used[0] += 1
        return pltpu.make_async_remote_copy(
            src_ref=src, dst_ref=dst, send_sem=send.at[i], recv_sem=recv.at[i],
            device_id=to, device_id_type=MESH,
        )

    pending = []

    def go(cp):
        cp.start()
        pending.append(cp)
        return cp

    def slot(ref, j):
        return ref.at[pl.ds(j * LEN, LEN)]

    def l_copy(e):
        return pltpu.make_async_remote_copy(
            src_ref=xp, dst_ref=lb.at[k], send_sem=lsend.at[e], recv_sem=lrecv.at[k],
            device_id=dev(yh, x, yl, (yh + e) % 2, z), device_id_type=MESH,
        )

    mine = jnp.logical_and(yh == yl, k == yl)
    l_local = pltpu.make_async_copy(xp, lb.at[k], lrecv.at[k])

    @pl.when(mine)
    def _():
        l_local.start()

    @pl.when(yh != yl)
    def _():
        l_copy(1).start()

    @pl.when(jnp.logical_not(mine))
    def _():
        l_copy(0).start()

    q1 = go(remote(q_ref, slot(qb, 1), xdev(1)))
    g2 = go(remote(g_ref, slot(gb, 2), xdev(3)))
    g1 = go(remote(g_ref, slot(gb, 1), xdev(1)))
    q2 = go(remote(q_ref, slot(qb, 2), xdev(3)))
    ks = go(remote(k_ref, slot(kb, 1), sib))
    vs = go(remote(v_ref, slot(vb, 1), sib))

    gf = g_ref[...].astype(F32)
    ones = jnp.ones((16, WIDE), BF16)

    def row_sums(o_ref):
        prod = gf * o_ref[...].astype(F32)
        hi = prod.astype(BF16)
        lo = (prod - hi.astype(F32)).astype(BF16)
        return (dot(ones, hi, NT) + dot(ones, lo, NT))[0:1]

    def position(yl_, x_, k_):
        return order_ref[(yl_ * 4 + x_) * 2 + k_].astype(F32)

    lam = jnp.full((1, LEN), lam_ref[0], F32)
    st[0, 0:1, :] = lse_ref[0] * LOG2E
    st[0, 1:2, :] = lse_ref[1] * LOG2E - jnp.log(lam) * LOG2E
    st[0, 2:3, :] = row_sums(o1_ref)
    st[0, 3:4, :] = row_sums(o2_ref)
    st[0, 4:5, :] = jnp.full((1, LEN), position(yl, x, k), F32)
    st[0, 5:8, :] = jnp.zeros((3, LEN), F32)
    gs = [go(remote(st.at[0], st.at[s], xdev(d))) for s, d in ((1, 1), (2, 3), (3, 2))]

    kp = go(remote(k_ref, slot(kb, 2), par))
    vp = go(remote(v_ref, slot(vb, 2), par))
    qb[0:LEN] = q_ref[...]
    gb[0:LEN] = g_ref[...]
    kb[0:LEN] = k_ref[...]
    vb[0:LEN] = v_ref[...]

    eye = (
        lax.broadcasted_iota(jnp.int32, (LEN, LEN), 0)
        == lax.broadcasted_iota(jnp.int32, (LEN, LEN), 1)
    ).astype(F32).astype(BF16)
    eye_wide = eye[0:WIDE, 0:WIDE]

    match = z % 2 == k
    soon = jnp.where(yh == yl, yl, 1 - yl)
    later = 1 - soon

    def z_copy(src, dst, pair, way):
        return pltpu.make_async_remote_copy(
            src_ref=zb.at[src, pair], dst_ref=zb.at[dst, pair],
            send_sem=zsend.at[dst, pair], recv_sem=zrecv.at[dst, pair],
            device_id=zdev(1 if way == 0 else 7), device_id_type=MESH,
        )

    def d_copy(i):
        return pltpu.make_async_remote_copy(
            src_ref=zb.at[i], dst_ref=sb.at[i], send_sem=dsend.at[i], recv_sem=drecv.at[i],
            device_id=sib, device_id_type=MESH,
        )

    def hand_over(places, far):
        @pl.when(match if far % 2 else jnp.logical_not(match))
        def _():
            for i in places:
                d_copy(i).start()

    def t_copy(pair):
        rows = pl.ds(pl.multiple_of((1 - k) * (LEN // 2), 32), LEN // 2)
        return pltpu.make_async_remote_copy(
            src_ref=tb.at[rows], dst_ref=zb.at[7, pair], send_sem=tsend.at[0],
            recv_sem=trecv.at[0], device_id=sib, device_id_type=MESH,
        )

    def z_turn():
        for b in range(2):
            pltpu.make_async_copy(xp, lb.at[b], lrecv.at[b]).wait()
        parts = [lb[b, :, i * LEN : (i + 1) * LEN] for b in range(2) for i in range(2)]
        tb[...] = dot(eye, jnp.concatenate(parts, axis=0), NT).astype(BF16)
        t_copy(k).start()
        zb[7, k] = tb[pl.ds(pl.multiple_of(k * (LEN // 2), 32), LEN // 2)]

    def z_begin(pair):
        @pl.when(pair == k)
        def _():
            z_turn()

        @pl.when(pair != k)
        def _():
            t_copy(1 - k).wait_recv()

        for way in range(2):
            z_copy(7, way, pair, way).start()

    def relay(far, pair):
        for way in range(2):
            place = 2 * (far - 1) + way
            z_copy(place, place, pair, way).wait_recv()
            if far < 3:
                z_copy(place, place + 2, pair, way).start()
            else:
                @pl.when(pair == way)
                def _():
                    z_copy(place, 6, pair, way).start()

    def finish_z():
        for way in range(2):
            z_copy(6, 6, way, way).wait_recv()
        hand_over((6,), 4)

    def ahead(f, *args):
        pl.when(yh == yl)(lambda: f(*args))

    def behind(f, *args):
        pl.when(yh != yl)(lambda: f(*args))

    def begin_later():
        z_begin(later)
        hand_over((7,), 0)

    def relay_later(far):
        relay(far, later)
        hand_over((2 * far - 2, 2 * far - 1), far)

    ahead(z_begin, soon)
    dkv[...] = jnp.zeros_like(dkv)
    dqt[...] = jnp.zeros_like(dqt)
    ks.wait_recv()
    kt[0] = dot(eye_wide, kb[0:PAIR], NT).astype(BF16)
    q1.wait_recv()
    q3 = go(remote(slot(qb, 1), slot(qb, 3), xdev(1)))

    @pl.when(yh == yl)
    def _():
        l_copy(1).start()

    g2.wait_recv()
    g3 = go(remote(slot(gb, 2), slot(gb, 3), xdev(3)))

    def attend(m, t):
        keys_at = slice(m * PAIR, (m + 1) * PAIR)
        tile = pl.ds(pl.multiple_of(t * TILE, TILE), TILE)
        qs, grads, stats = qb[tile], gb[tile], stp[t]
        keys = kb[keys_at]
        up = dot(vb[keys_at], grads, NT)
        score1 = dot(keys[:, :HALF], qs[:, :HALF], NT)
        score2 = dot(keys[:, HALF:], qs[:, HALF:], NT)
        s1, s2, mix = [], [], []
        for b in range(2):
            part = slice(b * LEN, (b + 1) * LEN)
            key_pos = position((yl + m) % 2, x, (k + b) % 2)
            hide = jnp.where(stats[4:5] < key_pos, 1e30, 0.0)
            p1 = jnp.exp2(score1[part] * (SCALE * LOG2E) - (stats[0:1] + hide))
            p2 = jnp.exp2(score2[part] * (SCALE * LOG2E) - (stats[1:2] + hide))
            if m == 0 and b == 0:
                key_row = lax.broadcasted_iota(jnp.int32, (LEN, TILE), 0)
                query_col = lax.broadcasted_iota(jnp.int32, (LEN, TILE), 1) + t * TILE
                p1 = jnp.where(key_row <= query_col, p1, 0.0)
                p2 = jnp.where(key_row <= query_col, p2, 0.0)
            s1.append((p1 * (up[part] - stats[2:3])).astype(BF16))
            s2.append((p2 * (up[part] - stats[3:4])).astype(BF16))
            mix.append((p1 - p2).astype(BF16))
        s1, s2, mix = (jnp.concatenate(a, axis=0) for a in (s1, s2, mix))
        dkv[keys_at, 0:HALF] += dot(s1, qs[:, :HALF])
        dkv[keys_at, HALF:WIDE] += dot(s2, qs[:, HALF:])
        dkv[keys_at, WIDE:] += dot(mix, grads)
        dqt[t, 0:HALF] += dot(kt[m, 0:HALF, :], s1)
        dqt[t, HALF:WIDE] += dot(kt[m, HALF:WIDE, :], s2)

    def sweep(m, low, high):
        def step(t, carry):
            attend(m, t)
            return carry

        lax.fori_loop(low, high, step, 0)

    def signed(t):
        sign = jnp.where(lax.broadcasted_iota(jnp.int32, (1, WIDE), 1) < HALF, SCALE, -SCALE)
        return t * sign

    def both_cores(j, i):
        sib_s[i] = dkv[j * LEN : (j + 1) * LEN].astype(BF16)
        return go(remote(sib_s.at[i], sib_r.at[i], sib))

    g1.wait_recv()
    gs[0].wait_recv()
    vs.wait_recv()
    behind(z_begin, soon)
    q2.wait_recv()
    gs[1].wait_recv()
    near = jnp.concatenate([st[0], st[1], st[2]], axis=1)
    for t in range(3):
        stp[t] = near[:, t * TILE : (t + 1) * TILE]
    sweep(0, 0, 2)
    ahead(relay, 1, soon)
    sweep(0, 2, 3)
    kp.wait_recv()
    rk = go(remote(slot(kb, 2), slot(kb, 3), sib))
    vp.wait_recv()
    rv = go(remote(slot(vb, 2), slot(vb, 3), sib))
    ahead(begin_later)
    behind(relay, 1, soon)
    rk.wait_recv()
    rv.wait_recv()
    kt[1] = dot(eye_wide, kb[PAIR:ALL], NT).astype(BF16)
    sweep(1, 0, 3)

    def turn_dq(t):
        dqf[t * TILE : (t + 1) * TILE] = dqt[t].T

    def send_dq(s, d):
        dqs[s - 1] = dqf[s * LEN : (s + 1) * LEN].astype(BF16)
        return go(remote(dqs.at[s - 1], dqr.at[s - 1], xdev(d)))

    for t in range(3):
        turn_dq(t)
    sq = [send_dq(1, 3)]
    ahead(relay, 2, soon)
    behind(begin_later)

    q3.wait_recv()
    g3.wait_recv()
    gs[2].wait_recv()
    far = jnp.concatenate([st[2], st[3]], axis=1)
    for t in (3, 4):
        stp[t] = far[:, t * TILE - 2 * LEN : (t + 1) * TILE - 2 * LEN]
    sweep(1, 3, 5)
    b0 = both_cores(3, 0)
    sweep(0, 3, 5)
    ahead(relay_later, 1)
    b1 = both_cores(1, 1)
    turn_dq(3)
    turn_dq(4)
    sq.append(send_dq(3, 2))
    sq.append(send_dq(2, 1))

    def rows_of(yl_, k_):
        return pl.ds(pl.multiple_of((yl_ * 2 + k_) * LEN, LEN), LEN)

    columns = (None, slice(0, WIDE), slice(WIDE, 2 * WIDE))

    def chip_sum(i, b):
        return dkv[2 * b * LEN : (2 * b + 1) * LEN, columns[i]] + sib_r[1 - b, :, columns[i]].astype(F32)

    def exchange(i, b):
        par_s[b, i - 1] = chip_sum(i, b).astype(BF16)
        return go(remote(par_s.at[b, i - 1], par_r.at[1 - b, i - 1], par))

    def total(i, b, came):
        came.wait_recv()
        value = chip_sum(i, b) + par_r[b, i - 1].astype(F32)
        value = (signed(value) if i == 1 else value).astype(BF16)
        ref = gw.at[i, rows_of(yl if b == 0 else 1 - yl, k)]
        ref[...] = value
        if b == 0:
            (dk_out if i == 1 else dv_out)[...] = value
        return go(remote(ref, ref, sib))

    b0.wait_recv()
    e1 = exchange(1, 1)
    b1.wait_recv()
    e0 = exchange(1, 0)
    behind(relay, 2, soon)
    f1 = exchange(2, 1)
    ahead(relay, 3, soon)
    c_own = total(1, 0, e1)
    behind(relay_later, 1)
    for cp in sq:
        cp.wait_recv()
    value = dqf[0:LEN]
    for i in range(3):
        value = value + dqr[i].astype(F32)
    value = signed(value).astype(BF16)
    dq_out[...] = value
    ref = gw.at[0, rows_of(yl, k)]
    ref[...] = value
    q_par = go(remote(ref, ref, par))
    q_sib = go(remote(ref, ref, sib))
    ahead(relay_later, 2)
    c_par = total(1, 1, e0)
    f0 = exchange(2, 0)
    behind(relay, 3, soon)

    def h_copy(i, way):
        return pltpu.make_async_remote_copy(
            src_ref=ws.at[2, i, pl.ds(way * (LEN // 2), LEN // 2)], dst_ref=hr.at[way, i],
            send_sem=hsend.at[way, i], recv_sem=hrecv.at[way, i],
            device_id=xdev(1 if way == 0 else 3), device_id_type=MESH,
        )

    def w_copy(i, way):
        return pltpu.make_async_remote_copy(
            src_ref=ws.at[way, i], dst_ref=wr.at[way, i],
            send_sem=wsend.at[way, i], recv_sem=wrecv.at[way, i],
            device_id=xdev(1 if way == 0 else 3), device_id_type=MESH,
        )

    def place_of(r):
        ahead = (2 * ((x + r) % 4) + k - z + 8) % 8
        place = jnp.where(ahead == 0, 7, 6)
        for far, at in ((1, 1), (7, 0), (2, 3), (6, 2), (3, 5), (5, 4)):
            place = jnp.where(ahead == far, at, place)
        return place

    own_half = pl.ds(pl.multiple_of(k * (LEN // 2), 32), LEN // 2)
    other_half = pl.ds(pl.multiple_of((1 - k) * (LEN // 2), 32), LEN // 2)

    def project(i, r):
        p = place_of(r)
        chunk = [jnp.concatenate([ref[p, 0], ref[p, 1]], axis=1) for ref in (zb, sb)]
        part = dot(jnp.concatenate(chunk, axis=0), gw[i])
        if r == 2:
            ws[2, i, own_half] = part[: LEN // 2].astype(BF16)
            ws[2, i, other_half] = part[LEN // 2 :].astype(BF16)
            for way in range(2):
                h_copy(i, way).start()
        else:
            to = w_out.at[i] if r == 0 else pp.at[r // 2, i]
            to[own_half] = part[: LEN // 2]
            to[other_half] = part[LEN // 2 :]

    def forward(i):
        for way in range(2):
            rows = slice(way * (LEN // 2), (way + 1) * (LEN // 2))
            rest = slice((1 - way) * (LEN // 2), (2 - way) * (LEN // 2))
            ws[way, i, rest] = pp[way, i, rest].astype(BF16)
            h_copy(i, way).wait_recv()
            ws[way, i, rows] = (pp[way, i, rows] + hr[way, i].astype(F32)).astype(BF16)
            w_copy(i, way).start()

    c_own.wait_recv()
    c_par.wait_recv()
    q_par.wait_recv()
    ref = gw.at[0, rows_of(1 - yl, k)]
    q_far = go(remote(ref, ref, sib))
    ahead(relay_later, 3)
    behind(relay_later, 2)
    q_sib.wait_recv()
    q_far.wait_recv()

    def first_sums():
        finish_z()
        for r in range(4):
            d_copy(place_of(r)).wait_recv()
        for r in (2, 1, 3):
            project(1, r)

    ahead(first_sums)
    c_own = total(2, 0, f1)
    c_par = total(2, 1, f0)
    behind(relay_later, 3)
    behind(first_sums)
    project(0, 2)
    forward(1)
    project(0, 1)
    project(0, 3)
    project(1, 0)
    c_own.wait_recv()
    c_par.wait_recv()
    project(2, 2)
    forward(0)
    project(2, 1)
    project(2, 3)
    project(0, 0)
    forward(2)
    project(2, 0)
    for i in (1, 0, 2):
        for way in range(2):
            w_copy(i, way).wait_recv()
        w_out[i] += wr[0, i].astype(F32) + wr[1, i].astype(F32)

    for cp in pending:
        cp.wait_send()

    @pl.when(jnp.logical_not(mine))
    def _():
        l_copy(0).wait_send()

    l_copy(1).wait_send()
    t_copy(k).wait_send()
    for place in range(6):
        for pair in range(2):
            z_copy(7, place, pair, 0).wait_send()
    for pair in range(2):
        z_copy(7, 6, pair, pair).wait_send()
    for far, places in ((0, (7,)), (1, (0, 1)), (2, (2, 3)), (3, (4, 5)), (4, (6,))):
        @pl.when(match if far % 2 else jnp.logical_not(match))
        def _():
            for i in places:
                d_copy(i).wait_send()

    for i in range(3):
        for way in range(2):
            h_copy(i, way).wait_send()
            w_copy(i, way).wait_send()


def tail(a, b, c, d, a_out, b_out, c_out, d_out, sems):
    copies = [
        pltpu.make_async_copy(src, dst, sems.at[i])
        for i, (src, dst) in enumerate(((d, d_out), (a, a_out), (b, b_out), (c, c_out)))
    ]
    for cp in copies:
        cp.start()
    for cp in copies:
        cp.wait()


def body(*args):
    vmem = pl.BlockSpec(memory_space=pltpu.VMEM)
    smem = pl.BlockSpec(memory_space=pltpu.SMEM)
    grad = jax.ShapeDtypeStruct((LEN, WIDE), BF16)
    dma = pltpu.SemaphoreType.DMA
    shapes = (grad, grad, grad, jax.ShapeDtypeStruct((3, LEN, WIDE), F32))
    results = pl.pallas_call(
        kernel,
        out_shape=shapes,
        in_specs=[vmem] * 8 + [smem] * 2,
        out_specs=(vmem,) * 4,
        scratch_shapes=[
            pltpu.VMEM((ALL, WIDE), BF16),
            pltpu.VMEM((ALL, WIDE), BF16),
            pltpu.VMEM((4, 8, LEN), F32),
            pltpu.VMEM((5, 8, TILE), F32),
            pltpu.VMEM((ALL, WIDE), BF16),
            pltpu.VMEM((ALL, WIDE), BF16),
            pltpu.VMEM((2, WIDE, PAIR), BF16),
            pltpu.VMEM((ALL, 2 * WIDE), F32),
            pltpu.VMEM((5, WIDE, TILE), F32),
            pltpu.VMEM((ALL, WIDE), F32),
            pltpu.VMEM((3, LEN, WIDE), BF16),
            pltpu.VMEM((3, LEN, WIDE), BF16),
            pltpu.VMEM((2, LEN, 2 * WIDE), BF16),
            pltpu.VMEM((2, LEN, 2 * WIDE), BF16),
            pltpu.VMEM((2, 2, LEN, WIDE), BF16),
            pltpu.VMEM((2, 2, LEN, WIDE), BF16),
            pltpu.VMEM((3, ALL, WIDE), BF16),
            pltpu.VMEM((LEN // 2, PAIR), BF16),
            pltpu.VMEM((2, LEN // 2, PAIR), BF16),
            pltpu.VMEM((LEN, PAIR), BF16),
            pltpu.VMEM((8, 2, LEN // 2, PAIR), BF16),
            pltpu.VMEM((8, 2, LEN // 2, PAIR), BF16),
            pltpu.VMEM((2, 3, LEN, WIDE), F32),
            pltpu.VMEM((2, 3, LEN // 2, WIDE), BF16),
            pltpu.VMEM((3, 3, LEN, WIDE), BF16),
            pltpu.VMEM((2, 3, LEN, WIDE), BF16),
            dma((32,)),
            dma((32,)),
            dma((7, 2)),
            dma((7, 2)),
            dma((8,)),
            dma((8,)),
            dma((1,)),
            dma((1,)),
            dma((2,)),
            dma((2,)),
            dma((2, 3)),
            dma((2, 3)),
            dma((2, 3)),
            dma((2, 3)),
        ],
        compiler_params=pltpu.CompilerParams(
            collective_id=0, has_side_effects=True, vmem_limit_bytes=56 * 2**20
        ),
        name="diff_attention_backward",
    )(*args)
    return pl.pallas_call(
        tail,
        out_shape=shapes,
        in_specs=[vmem] * 4,
        out_specs=(pl.BlockSpec(memory_space=pl.ANY),) * 4,
        scratch_shapes=[dma((4,))],
        name="write_results",
    )(*results)


def solution(mesh):
    in_specs = (P("ctx", "head"),) * 7 + (P(None, "head", "ctx"), P("head"), P())
    out_specs = (P("ctx", "head"), P("ctx", "head"), P("ctx", "head"), P(None, "ctx", "head"))
    return jax.shard_map(body, mesh=mesh, in_specs=in_specs, out_specs=out_specs, check_vma=False)
```

```python
import functools
import math

import jax
import jax.numpy as jnp
from jax import lax
from jax.experimental import pallas as pl
from jax.experimental.pallas import tpu as pltpu
from jax.sharding import PartitionSpec as P

HALF = 128
WIDE = 256
LEN = 320
PAIR = 640
TILE = 256
ALL = 1280
SCALE = 0.08838834764831845
LOG2E = 1.4426950408889634
F32 = jnp.float32
BF16 = jnp.bfloat16
MESH = pl.DeviceIdType.MESH

NN = (((1,), (0,)), ((), ()))
NT = (((1,), (1,)), ((), ()))


def dot(a, b, dims=NN):
    return lax.dot_general(a, b, dims, preferred_element_type=F32)


def kernel(
    x_ref, q_ref, k_ref, v_ref, o1_ref, o2_ref, g_ref, lse_ref, lam_ref, order_ref,
    dq_out, dk_out, dv_out, w_out,
    qb, gb, st, stp, kb, vb, kt, dkv, dqt, dqf,
    dqs, dqr, sib_s, sib_r, par_s, par_r, gw, xp, lb, tb, zb, sb, pp, hr, ws, wr,
    send, recv, zsend, zrecv, dsend, drecv, tsend, trecv, lsend, lrecv, hsend, hrecv, wsend, wrecv,
):
    c = lax.axis_index("ctx")
    h = lax.axis_index("head")
    yl, x, k = c // 8, (c // 2) % 4, c % 2
    yh, z = h // 8, h % 8

    def dev(yl_, x_, k_, yh_, z_):
        return ((yl_ * 4 + x_) * 2 + k_, yh_ * 8 + z_)

    def xdev(d):
        return dev(yl, (x + d) % 4, k, yh, z)

    def zdev(d):
        return dev(yl, x, k, yh, (z + d) % 8)

    sib = dev(yl, x, 1 - k, yh, z)
    par = dev(1 - yl, x, k, yh, z)

    barrier = pltpu.get_barrier_semaphore()
    partners = [xdev(1), xdev(2), xdev(3), zdev(1), zdev(7)]
    for a in range(2):
        for b in range(2):
            for e in range(2):
                if a + b + e > 0:
                    partners.append(dev((yl + a) % 2, x, (k + b) % 2, (yh + e) % 2, z))
    for p in partners:
        pl.semaphore_signal(barrier, inc=1, device_id=p, device_id_type=MESH)
    xp[...] = jnp.concatenate([x_ref[0 : LEN // 2], x_ref[LEN // 2 : LEN]], axis=1)
    pl.semaphore_wait(barrier, len(partners))

    used = [0]

    def remote(src, dst, to):
        i = used[0]
        used[0] += 1
        return pltpu.make_async_remote_copy(
            src_ref=src, dst_ref=dst, send_sem=send.at[i], recv_sem=recv.at[i],
            device_id=to, device_id_type=MESH,
        )

    pending = []

    def go(cp):
        cp.start()
        pending.append(cp)
        return cp

    def slot(ref, j):
        return ref.at[pl.ds(j * LEN, LEN)]

    def l_copy(e):
        return pltpu.make_async_remote_copy(
            src_ref=xp, dst_ref=lb.at[k], send_sem=lsend.at[e], recv_sem=lrecv.at[k],
            device_id=dev(yh, x, yl, (yh + e) % 2, z), device_id_type=MESH,
        )

    mine = jnp.logical_and(yh == yl, k == yl)
    l_local = pltpu.make_async_copy(xp, lb.at[k], lrecv.at[k])

    @pl.when(mine)
    def _():
        l_local.start()

    @pl.when(yh != yl)
    def _():
        l_copy(1).start()

    @pl.when(jnp.logical_not(mine))
    def _():
        l_copy(0).start()

    q1 = go(remote(q_ref, slot(qb, 1), xdev(1)))
    g2 = go(remote(g_ref, slot(gb, 2), xdev(3)))
    g1 = go(remote(g_ref, slot(gb, 1), xdev(1)))
    q2 = go(remote(q_ref, slot(qb, 2), xdev(3)))
    ks = go(remote(k_ref, slot(kb, 1), sib))
    vs = go(remote(v_ref, slot(vb, 1), sib))

    gf = g_ref[...].astype(F32)
    ones = jnp.ones((16, WIDE), BF16)

    def row_sums(o_ref):
        prod = gf * o_ref[...].astype(F32)
        hi = prod.astype(BF16)
        lo = (prod - hi.astype(F32)).astype(BF16)
        return (dot(ones, hi, NT) + dot(ones, lo, NT))[0:1]

    def position(yl_, x_, k_):
        return order_ref[(yl_ * 4 + x_) * 2 + k_].astype(F32)

    lam = jnp.full((1, LEN), lam_ref[0], F32)
    st[0, 0:1, :] = lse_ref[0] * LOG2E
    st[0, 1:2, :] = lse_ref[1] * LOG2E - jnp.log(lam) * LOG2E
    st[0, 2:3, :] = row_sums(o1_ref)
    st[0, 3:4, :] = row_sums(o2_ref)
    st[0, 4:5, :] = jnp.full((1, LEN), position(yl, x, k), F32)
    st[0, 5:8, :] = jnp.zeros((3, LEN), F32)
    gs = [go(remote(st.at[0], st.at[s], xdev(d))) for s, d in ((1, 1), (2, 3), (3, 2))]

    kp = go(remote(k_ref, slot(kb, 2), par))
    vp = go(remote(v_ref, slot(vb, 2), par))
    qb[0:LEN] = q_ref[...]
    gb[0:LEN] = g_ref[...]
    kb[0:LEN] = k_ref[...]
    vb[0:LEN] = v_ref[...]

    eye = (
        lax.broadcasted_iota(jnp.int32, (LEN, LEN), 0)
        == lax.broadcasted_iota(jnp.int32, (LEN, LEN), 1)
    ).astype(F32).astype(BF16)
    eye_wide = eye[0:WIDE, 0:WIDE]

    match = z % 2 == k
    soon = jnp.where(yh == yl, yl, 1 - yl)
    later = 1 - soon

    def z_copy(src, dst, pair, way):
        return pltpu.make_async_remote_copy(
            src_ref=zb.at[src, pair], dst_ref=zb.at[dst, pair],
            send_sem=zsend.at[dst, pair], recv_sem=zrecv.at[dst, pair],
            device_id=zdev(1 if way == 0 else 7), device_id_type=MESH,
        )

    def d_copy(i):
        return pltpu.make_async_remote_copy(
            src_ref=zb.at[i], dst_ref=sb.at[i], send_sem=dsend.at[i], recv_sem=drecv.at[i],
            device_id=sib, device_id_type=MESH,
        )

    def hand_over(places, far):
        @pl.when(match if far % 2 else jnp.logical_not(match))
        def _():
            for i in places:
                d_copy(i).start()

    def t_copy(pair):
        rows = pl.ds(pl.multiple_of((1 - k) * (LEN // 2), 32), LEN // 2)
        return pltpu.make_async_remote_copy(
            src_ref=tb.at[rows], dst_ref=zb.at[7, pair], send_sem=tsend.at[0],
            recv_sem=trecv.at[0], device_id=sib, device_id_type=MESH,
        )

    def z_turn():
        for b in range(2):
            pltpu.make_async_copy(xp, lb.at[b], lrecv.at[b]).wait()
        parts = [lb[b, :, i * LEN : (i + 1) * LEN] for b in range(2) for i in range(2)]
        tb[...] = dot(eye, jnp.concatenate(parts, axis=0), NT).astype(BF16)
        t_copy(k).start()
        zb[7, k] = tb[pl.ds(pl.multiple_of(k * (LEN // 2), 32), LEN // 2)]

    def z_begin(pair):
        @pl.when(pair == k)
        def _():
            z_turn()

        @pl.when(pair != k)
        def _():
            t_copy(1 - k).wait_recv()

        for way in range(2):
            z_copy(7, way, pair, way).start()

    def relay(far, pair):
        for way in range(2):
            place = 2 * (far - 1) + way
            z_copy(place, place, pair, way).wait_recv()
            if far < 3:
                z_copy(place, place + 2, pair, way).start()
            else:
                @pl.when(pair == way)
                def _():
                    z_copy(place, 6, pair, way).start()

    def finish_z():
        for way in range(2):
            z_copy(6, 6, way, way).wait_recv()
        hand_over((6,), 4)

    def ahead(f, *args):
        pl.when(yh == yl)(lambda: f(*args))

    def behind(f, *args):
        pl.when(yh != yl)(lambda: f(*args))

    def begin_later():
        z_begin(later)
        hand_over((7,), 0)

    def relay_later(far):
        relay(far, later)
        hand_over((2 * far - 2, 2 * far - 1), far)

    ahead(z_begin, soon)
    dkv[...] = jnp.zeros_like(dkv)
    dqt[...] = jnp.zeros_like(dqt)
    ks.wait_recv()
    kt[0] = dot(eye_wide, kb[0:PAIR], NT).astype(BF16)
    q1.wait_recv()
    q3 = go(remote(slot(qb, 1), slot(qb, 3), xdev(1)))

    @pl.when(yh == yl)
    def _():
        l_copy(1).start()

    g2.wait_recv()
    g3 = go(remote(slot(gb, 2), slot(gb, 3), xdev(3)))

    def attend(m, t):
        keys_at = slice(m * PAIR, (m + 1) * PAIR)
        tile = pl.ds(pl.multiple_of(t * TILE, TILE), TILE)
        qs, grads, stats = qb[tile], gb[tile], stp[t]
        keys = kb[keys_at]
        up = dot(vb[keys_at], grads, NT)
        score1 = dot(keys[:, :HALF], qs[:, :HALF], NT)
        score2 = dot(keys[:, HALF:], qs[:, HALF:], NT)
        s1, s2, mix = [], [], []
        for b in range(2):
            part = slice(b * LEN, (b + 1) * LEN)
            key_pos = position((yl + m) % 2, x, (k + b) % 2)
            hide = jnp.where(stats[4:5] < key_pos, 1e30, 0.0)
            p1 = jnp.exp2(score1[part] * (SCALE * LOG2E) - (stats[0:1] + hide))
            p2 = jnp.exp2(score2[part] * (SCALE * LOG2E) - (stats[1:2] + hide))
            if m == 0 and b == 0:
                key_row = lax.broadcasted_iota(jnp.int32, (LEN, TILE), 0)
                query_col = lax.broadcasted_iota(jnp.int32, (LEN, TILE), 1) + t * TILE
                p1 = jnp.where(key_row <= query_col, p1, 0.0)
                p2 = jnp.where(key_row <= query_col, p2, 0.0)
            s1.append((p1 * (up[part] - stats[2:3])).astype(BF16))
            s2.append((p2 * (up[part] - stats[3:4])).astype(BF16))
            mix.append((p1 - p2).astype(BF16))
        s1, s2, mix = (jnp.concatenate(a, axis=0) for a in (s1, s2, mix))
        dkv[keys_at, 0:HALF] += dot(s1, qs[:, :HALF])
        dkv[keys_at, HALF:WIDE] += dot(s2, qs[:, HALF:])
        dkv[keys_at, WIDE:] += dot(mix, grads)
        dqt[t, 0:HALF] += dot(kt[m, 0:HALF, :], s1)
        dqt[t, HALF:WIDE] += dot(kt[m, HALF:WIDE, :], s2)

    def sweep(m, low, high):
        def step(t, carry):
            attend(m, t)
            return carry

        lax.fori_loop(low, high, step, 0)

    def signed(t):
        sign = jnp.where(lax.broadcasted_iota(jnp.int32, (1, WIDE), 1) < HALF, SCALE, -SCALE)
        return t * sign

    def both_cores(j, i):
        sib_s[i] = dkv[j * LEN : (j + 1) * LEN].astype(BF16)
        return go(remote(sib_s.at[i], sib_r.at[i], sib))

    g1.wait_recv()
    gs[0].wait_recv()
    vs.wait_recv()
    behind(z_begin, soon)
    q2.wait_recv()
    gs[1].wait_recv()
    near = jnp.concatenate([st[0], st[1], st[2]], axis=1)
    for t in range(3):
        stp[t] = near[:, t * TILE : (t + 1) * TILE]
    sweep(0, 0, 2)
    ahead(relay, 1, soon)
    sweep(0, 2, 3)
    kp.wait_recv()
    rk = go(remote(slot(kb, 2), slot(kb, 3), sib))
    vp.wait_recv()
    rv = go(remote(slot(vb, 2), slot(vb, 3), sib))
    ahead(begin_later)
    behind(relay, 1, soon)
    rk.wait_recv()
    rv.wait_recv()
    kt[1] = dot(eye_wide, kb[PAIR:ALL], NT).astype(BF16)
    sweep(1, 0, 3)

    def turn_dq(t):
        dqf[t * TILE : (t + 1) * TILE] = dqt[t].T

    def send_dq(s, d):
        dqs[s - 1] = dqf[s * LEN : (s + 1) * LEN].astype(BF16)
        return go(remote(dqs.at[s - 1], dqr.at[s - 1], xdev(d)))

    for t in range(3):
        turn_dq(t)
    sq = [send_dq(1, 3)]
    ahead(relay, 2, soon)
    behind(begin_later)

    q3.wait_recv()
    g3.wait_recv()
    gs[2].wait_recv()
    far = jnp.concatenate([st[2], st[3]], axis=1)
    for t in (3, 4):
        stp[t] = far[:, t * TILE - 2 * LEN : (t + 1) * TILE - 2 * LEN]
    sweep(1, 3, 5)
    b0 = both_cores(3, 0)
    sweep(0, 3, 5)
    ahead(relay_later, 1)
    b1 = both_cores(1, 1)
    turn_dq(3)
    turn_dq(4)
    sq.append(send_dq(3, 2))
    sq.append(send_dq(2, 1))

    def rows_of(yl_, k_):
        return pl.ds(pl.multiple_of((yl_ * 2 + k_) * LEN, LEN), LEN)

    columns = (None, slice(0, WIDE), slice(WIDE, 2 * WIDE))

    def chip_sum(i, b):
        return dkv[2 * b * LEN : (2 * b + 1) * LEN, columns[i]] + sib_r[1 - b, :, columns[i]].astype(F32)

    def exchange(i, b):
        par_s[b, i - 1] = chip_sum(i, b).astype(BF16)
        return go(remote(par_s.at[b, i - 1], par_r.at[1 - b, i - 1], par))

    def total(i, b, came):
        came.wait_recv()
        value = chip_sum(i, b) + par_r[b, i - 1].astype(F32)
        value = (signed(value) if i == 1 else value).astype(BF16)
        ref = gw.at[i, rows_of(yl if b == 0 else 1 - yl, k)]
        ref[...] = value
        if b == 0:
            (dk_out if i == 1 else dv_out)[...] = value
        return go(remote(ref, ref, sib))

    b0.wait_recv()
    e1 = exchange(1, 1)
    b1.wait_recv()
    e0 = exchange(1, 0)
    behind(relay, 2, soon)
    f1 = exchange(2, 1)
    ahead(relay, 3, soon)
    c_own = total(1, 0, e1)
    behind(relay_later, 1)
    for cp in sq:
        cp.wait_recv()
    value = dqf[0:LEN]
    for i in range(3):
        value = value + dqr[i].astype(F32)
    value = signed(value).astype(BF16)
    dq_out[...] = value
    ref = gw.at[0, rows_of(yl, k)]
    ref[...] = value
    q_par = go(remote(ref, ref, par))
    q_sib = go(remote(ref, ref, sib))
    ahead(relay_later, 2)
    c_par = total(1, 1, e0)
    f0 = exchange(2, 0)
    behind(relay, 3, soon)

    def h_copy(i, way):
        return pltpu.make_async_remote_copy(
            src_ref=ws.at[2, i, pl.ds(way * (LEN // 2), LEN // 2)], dst_ref=hr.at[way, i],
            send_sem=hsend.at[way, i], recv_sem=hrecv.at[way, i],
            device_id=xdev(1 if way == 0 else 3), device_id_type=MESH,
        )

    def w_copy(i, way):
        return pltpu.make_async_remote_copy(
            src_ref=ws.at[way, i], dst_ref=wr.at[way, i],
            send_sem=wsend.at[way, i], recv_sem=wrecv.at[way, i],
            device_id=xdev(1 if way == 0 else 3), device_id_type=MESH,
        )

    def place_of(r):
        ahead = (2 * ((x + r) % 4) + k - z + 8) % 8
        place = jnp.where(ahead == 0, 7, 6)
        for far, at in ((1, 1), (7, 0), (2, 3), (6, 2), (3, 5), (5, 4)):
            place = jnp.where(ahead == far, at, place)
        return place

    own_half = pl.ds(pl.multiple_of(k * (LEN // 2), 32), LEN // 2)
    other_half = pl.ds(pl.multiple_of((1 - k) * (LEN // 2), 32), LEN // 2)

    def project(i, r):
        p = place_of(r)
        chunk = [jnp.concatenate([ref[p, 0], ref[p, 1]], axis=1) for ref in (zb, sb)]
        part = dot(jnp.concatenate(chunk, axis=0), gw[i])
        if r == 2:
            ws[2, i, own_half] = part[: LEN // 2].astype(BF16)
            ws[2, i, other_half] = part[LEN // 2 :].astype(BF16)
            for way in range(2):
                h_copy(i, way).start()
        else:
            to = w_out.at[i] if r == 0 else pp.at[r // 2, i]
            to[own_half] = part[: LEN // 2]
            to[other_half] = part[LEN // 2 :]

    def forward(i):
        for way in range(2):
            rows = slice(way * (LEN // 2), (way + 1) * (LEN // 2))
            rest = slice((1 - way) * (LEN // 2), (2 - way) * (LEN // 2))
            ws[way, i, rest] = pp[way, i, rest].astype(BF16)
            h_copy(i, way).wait_recv()
            ws[way, i, rows] = (pp[way, i, rows] + hr[way, i].astype(F32)).astype(BF16)
            w_copy(i, way).start()

    c_own.wait_recv()
    c_par.wait_recv()
    q_par.wait_recv()
    ref = gw.at[0, rows_of(1 - yl, k)]
    q_far = go(remote(ref, ref, sib))
    ahead(relay_later, 3)
    behind(relay_later, 2)
    q_sib.wait_recv()
    q_far.wait_recv()

    def first_sums():
        finish_z()
        for r in range(4):
            d_copy(place_of(r)).wait_recv()
        for r in (2, 1, 3):
            project(1, r)

    ahead(first_sums)
    c_own = total(2, 0, f1)
    c_par = total(2, 1, f0)
    behind(relay_later, 3)
    behind(first_sums)
    project(0, 2)
    forward(1)
    project(0, 1)
    project(0, 3)
    project(1, 0)
    c_own.wait_recv()
    c_par.wait_recv()
    project(2, 2)
    forward(0)
    project(2, 1)
    project(2, 3)
    project(0, 0)
    forward(2)
    project(2, 0)
    for i in (1, 0, 2):
        for way in range(2):
            w_copy(i, way).wait_recv()
        w_out[i] += wr[0, i].astype(F32) + wr[1, i].astype(F32)

    for cp in pending:
        cp.wait_send()

    @pl.when(jnp.logical_not(mine))
    def _():
        l_copy(0).wait_send()

    l_copy(1).wait_send()
    t_copy(k).wait_send()
    for place in range(6):
        for pair in range(2):
            z_copy(7, place, pair, 0).wait_send()
    for pair in range(2):
        z_copy(7, 6, pair, pair).wait_send()
    for far, places in ((0, (7,)), (1, (0, 1)), (2, (2, 3)), (3, (4, 5)), (4, (6,))):
        @pl.when(match if far % 2 else jnp.logical_not(match))
        def _():
            for i in places:
                d_copy(i).wait_send()

    for i in range(3):
        for way in range(2):
            h_copy(i, way).wait_send()
            w_copy(i, way).wait_send()


def tail(a, b, c, d, a_out, b_out, c_out, d_out):
    for src, dst in ((a, a_out), (b, b_out), (c, c_out), (d, d_out)):
        dst[...] = src[...]


def body(*args):
    vmem = pl.BlockSpec(memory_space=pltpu.VMEM)
    smem = pl.BlockSpec(memory_space=pltpu.SMEM)
    grad = jax.ShapeDtypeStruct((LEN, WIDE), BF16)
    dma = pltpu.SemaphoreType.DMA
    shapes = (grad, grad, grad, jax.ShapeDtypeStruct((3, LEN, WIDE), F32))
    results = pl.pallas_call(
        kernel,
        out_shape=shapes,
        in_specs=[vmem] * 8 + [smem] * 2,
        out_specs=(vmem,) * 4,
        scratch_shapes=[
            pltpu.VMEM((ALL, WIDE), BF16),
            pltpu.VMEM((ALL, WIDE), BF16),
            pltpu.VMEM((4, 8, LEN), F32),
            pltpu.VMEM((5, 8, TILE), F32),
            pltpu.VMEM((ALL, WIDE), BF16),
            pltpu.VMEM((ALL, WIDE), BF16),
            pltpu.VMEM((2, WIDE, PAIR), BF16),
            pltpu.VMEM((ALL, 2 * WIDE), F32),
            pltpu.VMEM((5, WIDE, TILE), F32),
            pltpu.VMEM((ALL, WIDE), F32),
            pltpu.VMEM((3, LEN, WIDE), BF16),
            pltpu.VMEM((3, LEN, WIDE), BF16),
            pltpu.VMEM((2, LEN, 2 * WIDE), BF16),
            pltpu.VMEM((2, LEN, 2 * WIDE), BF16),
            pltpu.VMEM((2, 2, LEN, WIDE), BF16),
            pltpu.VMEM((2, 2, LEN, WIDE), BF16),
            pltpu.VMEM((3, ALL, WIDE), BF16),
            pltpu.VMEM((LEN // 2, PAIR), BF16),
            pltpu.VMEM((2, LEN // 2, PAIR), BF16),
            pltpu.VMEM((LEN, PAIR), BF16),
            pltpu.VMEM((8, 2, LEN // 2, PAIR), BF16),
            pltpu.VMEM((8, 2, LEN // 2, PAIR), BF16),
            pltpu.VMEM((2, 3, LEN, WIDE), F32),
            pltpu.VMEM((2, 3, LEN // 2, WIDE), BF16),
            pltpu.VMEM((3, 3, LEN, WIDE), BF16),
            pltpu.VMEM((2, 3, LEN, WIDE), BF16),
            dma((32,)),
            dma((32,)),
            dma((7, 2)),
            dma((7, 2)),
            dma((8,)),
            dma((8,)),
            dma((1,)),
            dma((1,)),
            dma((2,)),
            dma((2,)),
            dma((2, 3)),
            dma((2, 3)),
            dma((2, 3)),
            dma((2, 3)),
        ],
        compiler_params=pltpu.CompilerParams(
            collective_id=0, has_side_effects=True, vmem_limit_bytes=56 * 2**20
        ),
        name="diff_attention_backward",
    )(*args)
    specs = [pl.BlockSpec((LEN // 2, WIDE), lambda i: (i, 0))] * 3
    specs.append(pl.BlockSpec((3, LEN // 2, WIDE), lambda i: (0, i, 0)))
    return pl.pallas_call(
        tail,
        out_shape=shapes,
        grid=(2,),
        in_specs=specs,
        out_specs=tuple(specs),
        compiler_params=pltpu.CompilerParams(vmem_limit_bytes=56 * 2**20),
        name="write_results",
    )(*results)


def solution(mesh):
    in_specs = (P("ctx", "head"),) * 7 + (P(None, "head", "ctx"), P("head"), P())
    out_specs = (P("ctx", "head"), P("ctx", "head"), P("ctx", "head"), P(None, "ctx", "head"))
    return jax.shard_map(body, mesh=mesh, in_specs=in_specs, out_specs=out_specs, check_vma=False)
```
